32 devices in a mesh: col: 4 (over z), tm: 8 (over y, x, core).
Axes of the slice: x: 2, y: 2, z: 4, core: 2. Of those that a mesh axis runs over, the one named last changes fastest.
Arguments:
- record: float32 [8192, 1024], P('tm', 'col'), as said below
- plan: int32 [3, 4], P(None, 'col'), may hold values 0 or 1
Outputs:
- rotated: float32 [8192, 1024], P('tm', 'col')
- column_rms: float32 [1024], P('col')
The draws below stay inside these ranges and needn't reach their ends.
Inputs may be any that keep to these rules, and one draw needn't show every extreme that they name: `record`: each column is independent noise scaled by a column factor and a time factor, plus a shared wave with a loading per column.
All inputs are finite; a program needn't handle non-finite values. No bound on the sum of `plan` on one device may be relied on, other than what follows from the above.
Results may differ from the reference program's by a relative error of at most 0.0003.
Values sent between devices are 32-bit elements; how exact they have to be, the bound alone decides.
No kernel may reach another device: no remote copies, remote signals or barrier semaphores. Data moves between devices by JAX's collectives and lax.ppermute only.
A program may use at most 64 MiB of HBM per device.

```python
import math
import jax
import jax.numpy as jnp
from jax import lax

BLOCK = 128
ROUNDS = 3
ROWS = 8192
COLS = 1024
N_COL = 4


def draw_record(key, part):
    key = jax.random.fold_in(key, 7)
    keys = jax.random.split(key, 5)
    noise = jax.random.normal(keys[0], (ROWS, COLS), jnp.float32)
    col_scale = jnp.exp(jax.random.uniform(keys[1], (COLS,), jnp.float32, math.log(0.3), math.log(3.0)))
    positions = jnp.arange(ROWS, dtype=jnp.float32) / ROWS
    row_scale = jnp.exp(math.log(3.0) * positions) * jnp.exp(jax.random.uniform(keys[2], (ROWS,), jnp.float32, 0.0, math.log(2.0)))
    wave = jax.random.normal(keys[3], (ROWS,), jnp.float32)
    loading = 0.5 * jax.random.normal(keys[4], (COLS,), jnp.float32)
    return noise * row_scale[:, None] * col_scale[None, :] + wave[:, None] * loading[None, :]


def place_ends(entries, own_key, low, top_value):
    spot = [jax.random.randint(jax.random.fold_in(own_key, axis), (), 0, length) for axis, length in enumerate(entries.shape)]
    longest = entries.shape.index(max(entries.shape))
    next_to = spot[:longest] + [(spot[longest] + 1) % entries.shape[longest]] + spot[longest + 1:]
    return entries.at[tuple(spot)].set(low).at[tuple(next_to)].set(top_value)


def setup_inputs(seed: int = 0) -> dict:
    key_of = jax.random.split(jax.random.key(seed), 3)
    return {
        "record": draw_record(jax.random.fold_in(key_of[2], 71), 0),
        "plan": place_ends((jax.random.randint(key_of[1], (ROUNDS, N_COL), 0, 2) < 1).astype(jnp.int32), jax.random.fold_in(key_of[1], 1), 0, 1),
    }


epsilon = 1e-06

def rotation(gram_mat):
    width = gram_mat.shape[0] // 2
    diagonal = jnp.diagonal(gram_mat)
    first_diag = diagonal[:width][:, None]
    second_diag = diagonal[width:][None, :]
    cross = gram_mat[:width, width:]
    difference = first_diag - second_diag
    ratio = cross * difference / (2.0 * (difference * difference + 4.0 * cross * cross + 0.01 * first_diag * second_diag))
    zeros = jnp.zeros((width, width), jnp.float32)
    skew = jnp.concatenate([jnp.concatenate([zeros, ratio], axis=1), jnp.concatenate([-ratio.T, zeros], axis=1)], axis=0)
    identity = jnp.eye(2 * width, dtype=jnp.float32)
    minus = identity - skew
    target = jnp.dot(minus, minus, precision=lax.Precision.HIGHEST)
    system = identity + jnp.dot(skew.T, skew, precision=lax.Precision.HIGHEST)
    factor = jnp.linalg.cholesky(system)
    middle = lax.linalg.triangular_solve(factor, target, left_side=True, lower=True)
    return lax.linalg.triangular_solve(factor, middle, left_side=True, lower=True, transpose_a=True)

def reference(record, plan):
    total_rows = record.shape[0]
    pair_cols = record.reshape(total_rows, N_COL, 2 * BLOCK)
    for step_index in range(ROUNDS):
        gram_all = jnp.einsum('mpi,mpj->pij', pair_cols, pair_cols, precision=lax.Precision.HIGHEST)
        turns = jax.vmap(rotation)(gram_all)
        turned = jnp.einsum('mpi,pij->mpj', pair_cols, turns, precision=lax.Precision.HIGHEST)
        first_block = turned[:, :, :BLOCK]
        second_block = turned[:, :, BLOCK:]
        moves_second = (plan[step_index] == 1)[None, :, None]
        moving = jnp.where(moves_second, second_block, first_block)
        staying = jnp.where(moves_second, first_block, second_block)
        incoming = jnp.roll(moving, 1, axis=1)
        pair_cols = jnp.concatenate([staying, incoming], axis=2)
    rotated = pair_cols.reshape(total_rows, COLS)
    energy = lax.optimization_barrier(jnp.sum(rotated * rotated, axis=0))
    column_rms = jnp.sqrt(energy / total_rows + epsilon)
    return (rotated, column_rms)
```

```python
import functools
import jax
import jax.numpy as jnp
from jax import lax
from jax.experimental import pallas as pl
from jax.experimental.pallas import tpu as pltpu
from jax.sharding import PartitionSpec as P

epsilon = 1e-06
F32 = jnp.float32
BF16 = jnp.bfloat16
NN = (((1,), (0,)), ((), ()))
NT = (((1,), (1,)), ((), ()))
TN = (((0,), (0,)), ((), ()))
VMEM = pl.BlockSpec(memory_space=pltpu.VMEM)
SMEM = pl.BlockSpec(memory_space=pltpu.SMEM)


def split(x):
    high = x.astype(BF16)
    return high, (x - high.astype(F32)).astype(BF16)


def dot3(a, b, dims=NN):
    one = functools.partial(lax.dot_general, dimension_numbers=dims, preferred_element_type=F32)
    return one(a[0], b[0]) + (one(a[0], b[1]) + one(a[1], b[0]))


def identity_of(width):
    shape = (width, width)
    return (lax.broadcasted_iota(jnp.int32, shape, 0) == lax.broadcasted_iota(jnp.int32, shape, 1)).astype(F32)


def gram_of(first, second):
    width = first.shape[1]
    cross = dot3(split(first), split(second), TN)
    tail = [
        jnp.sum(first * first, axis=0, keepdims=True),
        jnp.sum(second * second, axis=0, keepdims=True),
        jnp.zeros((6, width), F32),
    ]
    return jnp.concatenate([cross] + tail, axis=0)


def inverse(skew, error_ref, total_ref):
    width = skew[0].shape[0]
    square = dot3(skew, skew, NT)
    bound = jnp.minimum(jnp.max(jnp.sum(jnp.abs(square), axis=0)), jnp.sqrt(jnp.sum(square * square)))
    identity = identity_of(width)
    scale = 2.0 / (bound + 2.0)
    error_ref[...] = (1.0 - scale) * identity - scale * square
    total_ref[...] = scale * identity

    def step(error_bound):
        grow = 2.0 / (2.0 - error_bound * error_bound)
        error, total = error_ref[...], total_ref[...]
        both = dot3(split(jnp.concatenate([error, total], axis=0)), split(error))
        total_ref[...] = grow * (total + both[width:])
        error_ref[...] = (1.0 - grow) * identity + grow * both[:width]
        return error_bound * error_bound / (2.0 - error_bound * error_bound)

    lax.while_loop(lambda error_bound: error_bound > 1e-3, step, bound / (bound + 2.0))
    total = total_ref[...]
    parts = split(total)
    residual = identity - total - dot3(split(square), parts)
    return total + dot3(parts, split(residual))


def rotated_halves(s_ref, first, second, error_ref, total_ref):
    skew = split(s_ref[...])
    inner = inverse(skew, error_ref, total_ref)
    mixed = dot3(split(first + dot3(split(second), skew, NT)), split(inner))
    return 2.0 * mixed - first, second - 2.0 * dot3(split(mixed), skew)


def gram_kernel(pair_ref, gram_ref):
    width = pair_ref.shape[1] // 2
    gram_ref[...] = gram_of(pair_ref[:, :width], pair_ref[:, width:])


def ratio_kernel(*refs):
    parts, s_ref = refs[:-1], refs[-1]
    gram = functools.reduce(lambda x, y: x + y, [ref[...] for ref in parts])
    width = gram.shape[1]
    cross, second_diag = gram[:width], gram[width + 1 : width + 2]
    first_diag = jnp.sum(identity_of(width) * gram[width : width + 1], axis=1, keepdims=True)
    difference = first_diag - second_diag
    s_ref[...] = (
        cross * difference / (2.0 * (difference * difference + 4.0 * cross * cross + 0.01 * first_diag * second_diag))
    )


def own_kernel(plan_ref, s_ref, pair_ref, staying_ref, error_ref, total_ref):
    width = s_ref.shape[0]
    first, second = rotated_halves(s_ref, pair_ref[:, :width], pair_ref[:, width:], error_ref, total_ref)
    staying_ref[...] = jnp.where(plan_ref[0] == 1, first, second)


def neighbour_kernel(last, halves, plan_ref, s_ref, staying_ref, *refs):
    width = s_ref.shape[0]
    if halves == 2:
        first, second = refs[0][...], refs[1][...]
        refs = refs[2:]
    else:
        first, second = refs[0][:, :width], refs[0][:, width:]
        refs = refs[1:]
    *outs, error_ref, total_ref = refs
    first, second = rotated_halves(s_ref, first, second, error_ref, total_ref)
    moves_second = plan_ref[0] == 1
    moving = jnp.where(moves_second, second, first)
    staying = staying_ref[...]
    pair_ref, gram_ref = outs[:2]
    pair_ref[:, :width] = staying
    pair_ref[:, width:] = moving
    if last:
        gram_ref[...] = jnp.concatenate(
            [
                jnp.sum(staying * staying, axis=0, keepdims=True),
                jnp.sum(moving * moving, axis=0, keepdims=True),
                jnp.zeros((6, width), F32),
            ],
            axis=0,
        )
    else:
        gram_ref[...] = gram_of(staying, moving)
        outs[2][...] = moving
        outs[3][...] = jnp.where(moves_second, first, second)


def call(kernel, operands, outs, scratch=(), plan=None, name=None):
    specs = [SMEM] * (plan is not None) + [VMEM] * len(operands)
    return pl.pallas_call(
        kernel,
        out_shape=[jax.ShapeDtypeStruct(shape, F32) for shape in outs],
        in_specs=specs,
        out_specs=[VMEM] * len(outs),
        scratch_shapes=list(scratch),
        compiler_params=pltpu.CompilerParams(vmem_limit_bytes=48 * 1024 * 1024),
        name=name,
    )(*([plan] if plan is not None else []), *operands)


def passed_along(block, axis):
    size = lax.axis_size(axis)
    return lax.ppermute(block, axis, [(i, (i + 1) % size) for i in range(size)])


def parts_of_sum(term, axis):
    size = lax.axis_size(axis)
    if size & (size - 1):
        return [lax.psum(term, axis)]
    parts, bit = [term], 1
    while bit < size:
        term = functools.reduce(lambda x, y: x + y, parts)
        masks = [bit] if bit == 1 or 2 * bit >= size else [bit, 2 * bit, 3 * bit]
        parts = [term] + [lax.ppermute(term, axis, [(i, i ^ mask) for i in range(size)]) for mask in masks]
        bit *= 2 if len(masks) == 1 else 4
    return parts


def body(record, plan):
    rows, width = record.shape[0], record.shape[1] // 2
    rounds = plan.shape[0]
    total_rows = rows * lax.axis_size("tm")
    square, block, gram = (width, width), (rows, width), (width + 8, width)
    scratch = [pltpu.VMEM(square, F32)] * 2
    pair = record
    neighbour = [passed_along(record, "col")]
    neighbour_plan = passed_along(plan, "col")
    (terms,) = call(gram_kernel, [pair], [gram], name="gram")
    for step in range(rounds):
        last = step + 1 == rounds
        (ratio,) = call(ratio_kernel, parts_of_sum(terms, "tm"), [square], name="ratio")
        neighbour_ratio = passed_along(ratio, "col")
        (staying,) = call(own_kernel, [ratio, pair], [block], scratch, plan[step], name="own")
        operands = [neighbour_ratio, staying] + neighbour
        if last:
            pair, terms = call(
                functools.partial(neighbour_kernel, True, len(neighbour)), operands, [record.shape, (8, width)], scratch, neighbour_plan[step], name="last"
            )
        else:
            pair, terms, moving, neighbour_staying = call(
                functools.partial(neighbour_kernel, False, len(neighbour)), operands, [record.shape, gram, block, block], scratch, neighbour_plan[step], name="both"
            )
            neighbour = [neighbour_staying, passed_along(moving, "col")]
    energy = functools.reduce(lambda x, y: x + y, parts_of_sum(terms, "tm"))[:2].reshape(2 * width)
    return (pair, jnp.sqrt(energy / total_rows + epsilon))


def solution(mesh):
    in_specs = (P("tm", "col"), P(None, "col"))
    out_specs = (P("tm", "col"), P("col"))
    return jax.shard_map(body, mesh=mesh, in_specs=in_specs, out_specs=out_specs, check_vma=False)
```

```python
import functools
import jax
import jax.numpy as jnp
from jax import lax
from jax.experimental import pallas as pl
from jax.experimental.pallas import tpu as pltpu
from jax.sharding import PartitionSpec as P

epsilon = 1e-06
MICROS = {"own": 1.0, "inverse": 2.0, "turn": 1.0, "join": 0.5}
F32 = jnp.float32
BF16 = jnp.bfloat16
NN = (((1,), (0,)), ((), ()))
NT = (((1,), (1,)), ((), ()))
TN = (((0,), (0,)), ((), ()))
VMEM = pl.BlockSpec(memory_space=pltpu.VMEM)


def split(x):
    high = x.astype(BF16)
    return high, (x - high.astype(F32)).astype(BF16)


def dot3(a, b, dims=NN):
    one = functools.partial(lax.dot_general, dimension_numbers=dims, preferred_element_type=F32)
    return one(a[0], b[0]) + (one(a[0], b[1]) + one(a[1], b[0]))


def identity_of(width):
    shape = (width, width)
    return (lax.broadcasted_iota(jnp.int32, shape, 0) == lax.broadcasted_iota(jnp.int32, shape, 1)).astype(F32)


def gram_of(first, second):
    width = first.shape[1]
    cross = dot3(split(first), split(second), TN)
    tail = [
        jnp.sum(first * first, axis=0, keepdims=True),
        jnp.sum(second * second, axis=0, keepdims=True),
        jnp.zeros((6, width), F32),
    ]
    return jnp.concatenate([cross] + tail, axis=0)


def inverse(skew, error_ref, total_ref):
    width = skew[0].shape[0]
    square = dot3(skew, skew, NT)
    bound = jnp.minimum(jnp.max(jnp.sum(jnp.abs(square), axis=0)), jnp.sqrt(jnp.sum(square * square)))
    identity = identity_of(width)
    scale = 2.0 / (bound + 2.0)
    error_ref[...] = (1.0 - scale) * identity - scale * square
    total_ref[...] = scale * identity

    def step(error_bound):
        grow = 2.0 / (2.0 - error_bound * error_bound)
        error, total = error_ref[...], total_ref[...]
        both = dot3(split(jnp.concatenate([error, total], axis=0)), split(error))
        total_ref[...] = grow * (total + both[width:])
        error_ref[...] = (1.0 - grow) * identity + grow * both[:width]
        return error_bound * error_bound / (2.0 - error_bound * error_bound)

    lax.while_loop(lambda error_bound: error_bound > 1e-3, step, bound / (bound + 2.0))
    total = total_ref[...]
    parts = split(total)
    residual = identity - total - dot3(split(square), parts)
    return total + dot3(parts, split(residual))


def rotated_halves(skew, inner, first, second):
    mixed = dot3(split(first + dot3(split(second), skew, NT)), split(inner))
    return 2.0 * mixed - first, second - 2.0 * dot3(split(mixed), skew)


def gram_kernel(pair_ref, gram_ref, head_ref):
    width = pair_ref.shape[1] // 2
    gram_ref[...] = gram_of(pair_ref[:, :width], pair_ref[:, width:])
    head_ref[...] = pair_ref[: head_ref.shape[0]]


def ratio_kernel(row, plan_ref, *refs):
    parts, s_ref = refs[:-1], refs[-1]
    gram = functools.reduce(lambda x, y: x + y, [ref[...] for ref in parts])
    width = gram.shape[1]
    cross, second_diag = gram[:width], gram[width + 1 : width + 2]
    first_diag = jnp.sum(identity_of(width) * gram[width : width + 1], axis=1, keepdims=True)
    difference = first_diag - second_diag
    s_ref[:width] = (
        cross * difference / (2.0 * (difference * difference + 4.0 * cross * cross + 0.01 * first_diag * second_diag))
    )
    s_ref[width:] = plan_ref[row : row + 8]


def own_kernel(known, kept, s_ref, pair_ref, staying_ref, *refs):
    *outs, error_ref, total_ref = refs
    width = s_ref.shape[1]
    skew = split(s_ref[:width])
    inner = inverse(skew, error_ref, total_ref)
    first, second = rotated_halves(skew, inner, pair_ref[:, :width], pair_ref[:, width:])
    moves_second = s_ref[width : width + 1] > 0.5
    staying = jnp.where(moves_second, first, second)
    staying_ref[...] = staying
    if known < pair_ref.shape[0]:
        outs[0][...] = jnp.where(moves_second, second[known:], first[known:])
    if known < kept:
        outs[-1][...] = staying[known:kept]


def inverse_kernel(s_ref, inner_ref, error_ref, total_ref):
    inner_ref[...] = inverse(split(s_ref[: s_ref.shape[1]]), error_ref, total_ref)


def turned(s_ref, inner_ref, refs):
    width = s_ref.shape[1]
    if len(refs) == 1:
        first, second = refs[0][:, :width], refs[0][:, width:]
    else:
        second = refs[1][...]
        first = jnp.concatenate([refs[0][...]] + [ref[...] for ref in refs[2:]], axis=0)
    first, second = rotated_halves(split(s_ref[:width]), inner_ref[...], first, second)
    moves_second = s_ref[width : width + 1] > 0.5
    return jnp.where(moves_second, second, first), jnp.where(moves_second, first, second)


def joined(staying, moving, pair_ref, gram_ref, kept):
    width = staying.shape[1]
    pair_ref[:, :width] = staying
    pair_ref[:, width:] = moving
    if kept:
        gram_ref[...] = gram_of(staying, moving)
    else:
        gram_ref[...] = jnp.concatenate(
            [
                jnp.sum(staying * staying, axis=0, keepdims=True),
                jnp.sum(moving * moving, axis=0, keepdims=True),
                jnp.zeros((6, width), F32),
            ],
            axis=0,
        )


def turn_kernel(parts, s_ref, inner_ref, *refs):
    moving, staying = turned(s_ref, inner_ref, refs[:parts])
    refs[parts][...] = moving
    if len(refs) > parts + 1:
        refs[parts + 1][...] = staying[: refs[parts + 1].shape[0]]


def join_kernel(kept, staying_ref, moving_ref, tail_ref, pair_ref, gram_ref, *outs):
    moving = jnp.concatenate([moving_ref[...], tail_ref[...]], axis=0)
    joined(staying_ref[...], moving, pair_ref, gram_ref, kept)
    if kept:
        outs[0][...] = moving[:kept]


def turn_join_kernel(kept, parts, s_ref, inner_ref, staying_ref, *refs):
    moving, neighbour_staying = turned(s_ref, inner_ref, refs[:parts])
    pair_ref, gram_ref, *outs = refs[parts:]
    joined(staying_ref[...], moving, pair_ref, gram_ref, kept)
    if kept:
        outs[0][...] = moving[:kept]
        outs[1][...] = neighbour_staying[: outs[1].shape[0]]


def call(kernel, operands, outs, scratch=(), name=""):
    micros = MICROS.get(name, 0.0)
    return pl.pallas_call(
        kernel,
        out_shape=[jax.ShapeDtypeStruct(shape, F32) for shape in outs],
        in_specs=[VMEM] * len(operands),
        out_specs=[VMEM] * len(outs),
        scratch_shapes=list(scratch),
        compiler_params=pltpu.CompilerParams(vmem_limit_bytes=48 * 1024 * 1024),
        cost_estimate=pl.CostEstimate(flops=int(micros * 1e9) + 1, bytes_accessed=int(micros * 3.5e6) + 1, transcendentals=0),
        name=name,
    )(*operands)


def passed_along(block, axis):
    size = lax.axis_size(axis)
    return lax.ppermute(block, axis, [(i, (i + 1) % size) for i in range(size)])


def parts_of_sum(term, axis):
    size = lax.axis_size(axis)
    if size & (size - 1):
        return [lax.psum(term, axis)]
    parts, bit = [term], 1
    while bit < size:
        term = functools.reduce(lambda x, y: x + y, parts)
        masks = [bit] if bit == 1 or 2 * bit >= size else [bit, 2 * bit, 3 * bit]
        parts = [term] + [lax.ppermute(term, axis, [(i, i ^ mask) for i in range(size)]) for mask in masks]
        bit *= 2 if len(masks) == 1 else 4
    return parts


def known_rows(rows, rounds):
    eighths = [5] + [6] * rounds
    return [rows * part // 128 * 16 for part in eighths[:rounds]] + [0]


def body(record, plan):
    rows, width = record.shape[0], record.shape[1] // 2
    rounds = plan.shape[0]
    total_rows = rows * lax.axis_size("tm")
    square, gram = (width, width), (width + 8, width)
    scratch = [pltpu.VMEM(square, F32)] * 2
    heads = known_rows(rows, rounds)
    pair = record
    terms, raw_head = call(gram_kernel, [pair], [gram, (heads[0], 2 * width)], name="gram")
    neighbour = [passed_along(raw_head, "col")]
    plan_rows = jnp.repeat(jnp.broadcast_to(plan.astype(F32), (rounds, width)), 8, axis=0)
    for step in range(rounds):
        known, kept = heads[step], heads[step + 1]
        parts = parts_of_sum(terms, "tm")
        (ratio,) = call(functools.partial(ratio_kernel, 8 * step), [plan_rows] + parts, [gram], name="ratio")
        neighbour_ratio = passed_along(ratio, "col")
        outs = [(rows, width)] + [(rows - known, width)] * (known < rows) + [(kept - known, width)] * (known < kept)
        staying, *sent = call(functools.partial(own_kernel, known, kept), [ratio, pair], outs, scratch, name="own")
        (inner,) = call(inverse_kernel, [neighbour_ratio], [square], scratch, name="inverse")
        turn = [neighbour_ratio, inner]
        sums = gram if kept else (8, width)
        kept_outs = [(kept, width)] * (kept > 0)
        known_outs = [(min(known, kept), width)] * (kept > 0)
        if known < rows:
            tail = passed_along(sent[0], "col")
            kernel = functools.partial(turn_kernel, len(neighbour))
            moving, *kept_staying = call(kernel, turn + neighbour, [(known, width)] + known_outs, name="turn")
            kernel = functools.partial(join_kernel, kept)
            pair, terms, *moving = call(kernel, [staying, moving, tail], [record.shape, sums] + kept_outs, name="join")
        else:
            tail = None
            kernel = functools.partial(turn_join_kernel, kept, len(neighbour))
            outs = [record.shape, sums] + kept_outs + known_outs
            pair, terms, *rest = call(kernel, turn + [staying] + neighbour, outs, name="both")
            moving, kept_staying = rest[:1], rest[1:]
        if kept:
            neighbour = kept_staying + [passed_along(moving[0], "col")]
        if known < kept:
            more = sent[-1]
            if tail is not None:
                more, _ = lax.optimization_barrier((more, tail))
            neighbour.append(passed_along(more, "col"))
    energy = functools.reduce(lambda x, y: x + y, parts_of_sum(terms, "tm"))[:2].reshape(2 * width)
    return (pair, jnp.sqrt(energy / total_rows + epsilon))


def solution(mesh):
    in_specs = (P("tm", "col"), P(None, "col"))
    out_specs = (P("tm", "col"), P("col"))
    return jax.shard_map(body, mesh=mesh, in_specs=in_specs, out_specs=out_specs, check_vma=False)
```

```python
import functools
import jax
import jax.numpy as jnp
from jax import lax
from jax.experimental import pallas as pl
from jax.experimental.pallas import tpu as pltpu
from jax.sharding import PartitionSpec as P

epsilon = 1e-06
MICROS = {"own": 1.0, "inverse": 2.0, "turn": 1.0, "join": 0.5}
F32 = jnp.float32
BF16 = jnp.bfloat16
NN = (((1,), (0,)), ((), ()))
NT = (((1,), (1,)), ((), ()))
TN = (((0,), (0,)), ((), ()))
VMEM = pl.BlockSpec(memory_space=pltpu.VMEM)


def split(x):
    high = x.astype(BF16)
    return high, (x - high.astype(F32)).astype(BF16)


def product(a, b, dims):
    return lax.dot_general(a, b, dims, preferred_element_type=F32)


def right(b, transposed=False):
    high, low = split(b)
    zeros = jnp.zeros_like(low)
    if transposed:
        return jnp.concatenate([jnp.concatenate([high, high], axis=1), jnp.concatenate([low, zeros], axis=1)], axis=0)
    return jnp.concatenate([jnp.concatenate([high, low], axis=1), jnp.concatenate([high, zeros], axis=1)], axis=0)


def times(a, b, transposed=False):
    both = product(jnp.concatenate(split(a), axis=1), b, NT if transposed else NN)
    half = both.shape[1] // 2
    return both[:, :half] + both[:, half:]


def across(a, b):
    both = product(jnp.concatenate(split(a), axis=1), jnp.concatenate(split(b), axis=1), TN)
    width = a.shape[1]
    return both[:width, :width] + (both[:width, width:] + both[width:, :width])


def identity_of(width):
    shape = (width, width)
    return (lax.broadcasted_iota(jnp.int32, shape, 0) == lax.broadcasted_iota(jnp.int32, shape, 1)).astype(F32)


def gram_of(first, second, whole):
    width = first.shape[1]
    parts = [
        across(first, second),
        jnp.sum(first * first, axis=0, keepdims=True),
        jnp.sum(second * second, axis=0, keepdims=True),
        jnp.zeros((6, width), F32),
    ]
    if whole:
        above, below = triangles(width)
        parts.append(
            jnp.where(above, across(first, first), 0.0)
            + jnp.where(below, across(second, second), 0.0)
        )
    return jnp.concatenate(parts, axis=0)


def triangles(width):
    row = lax.broadcasted_iota(jnp.int32, (width, width), 0)
    column = lax.broadcasted_iota(jnp.int32, (width, width), 1)
    return row < column, row > column


def whole_gram(gram):
    width = gram.shape[1]
    above, below = triangles(width)
    identity = identity_of(width)
    cross, packed = gram[:width], gram[width + 8 :]
    blocks = []
    for triangle, diagonal in ((above, gram[width : width + 1]), (below, gram[width + 1 : width + 2])):
        half = jnp.where(triangle, packed, 0.0)
        blocks.append(half + half.T + identity * diagonal)
    return jnp.concatenate([blocks[0], cross.T], axis=0), jnp.concatenate([cross, blocks[1]], axis=0)


def inverse(skew, error_ref, total_ref):
    width = skew.shape[0]
    identity = identity_of(width)
    square = times(skew, right(skew, True), True)
    bound = jnp.minimum(
        jnp.max(jnp.sum(jnp.abs(square), axis=0, keepdims=True), axis=1, keepdims=True),
        jnp.sqrt(jnp.sum(jnp.sum(square * square, axis=0, keepdims=True), axis=1, keepdims=True)),
    )
    scale = 2.0 / (bound + 2.0)
    error_bound = bound / (bound + 2.0)
    error = (1.0 - scale) * identity - scale * square
    total = scale * identity
    for step in range(4):
        grow = 2.0 / (2.0 - error_bound * error_bound)
        if step == 0:
            total, error = (grow * scale) * (identity + error), times(error, right(error))
        else:
            both = times(jnp.concatenate([error, total], axis=0), right(error))
            total, error = grow * (total + both[width:]), both[:width]
        error = (1.0 - grow) * identity + grow * error
        error_bound = error_bound * error_bound / (2.0 - error_bound * error_bound)
    total_ref[...] = total + times(total, right(identity - total - times(square, right(total))))

    @pl.when(error_bound[0, 0] > 1e-3)
    def _():
        exact = functools.partial(lax.dot_general, precision=lax.Precision.HIGHEST, preferred_element_type=F32)
        square = exact(skew, skew, NT)
        error_ref[...] = (1.0 - scale) * identity - scale * square
        total_ref[...] = scale * identity

        def more(error_bound):
            grow = 2.0 / (2.0 - error_bound * error_bound)
            error, total = error_ref[...], total_ref[...]
            total_ref[...] = grow * (total + exact(total, error, NN))
            error_ref[...] = (1.0 - grow) * identity + grow * exact(error, error, NN)
            return error_bound * error_bound / (2.0 - error_bound * error_bound)

        lax.while_loop(lambda error_bound: error_bound > 1e-4, more, (bound / (bound + 2.0))[0, 0])
        for _ in range(2):
            total = total_ref[...]
            total_ref[...] = total + exact(total, identity - total - exact(square, total, NN), NN)

    return total_ref[...]


def rotated_halves(skew, inner, first, second):
    mixed = times(first + times(second, right(skew, True), True), right(inner))
    return 2.0 * mixed - first, second - 2.0 * times(mixed, right(skew))


def gram_kernel(pair_ref, gram_ref, head_ref):
    width = pair_ref.shape[1] // 2
    gram_ref[...] = gram_of(pair_ref[:, :width], pair_ref[:, width:], gram_ref.shape[0] > width + 8)
    head_ref[...] = pair_ref[: head_ref.shape[0]]


def ratio_kernel(row, count, plan_ref, *refs):
    parts, (s_ref, *sum_ref) = refs[:count], refs[count:]
    gram = functools.reduce(lambda x, y: x + y, [ref[...] for ref in parts])
    if sum_ref:
        sum_ref[0][...] = gram
    width = gram.shape[1]
    cross, second_diag = gram[:width], gram[width + 1 : width + 2]
    first_diag = jnp.sum(identity_of(width) * gram[width : width + 1], axis=1, keepdims=True)
    difference = first_diag - second_diag
    s_ref[:width] = (
        cross * difference / (2.0 * (difference * difference + 4.0 * cross * cross + 0.01 * first_diag * second_diag))
    )
    s_ref[width:] = plan_ref[row : row + 8]


def own_kernel(known, kept, last, s_ref, pair_ref, *refs):
    *refs, error_ref, total_ref = refs
    width = s_ref.shape[1]
    rows = pair_ref.shape[0]
    skew = s_ref[:width]
    inner = inverse(skew, error_ref, total_ref)
    moves_second = s_ref[width : width + 1] > 0.5
    first, second = pair_ref[:, :width], pair_ref[:, width:]
    if last:
        gram_ref, *refs = refs
        identity, zeros = identity_of(width), jnp.zeros((width, width), F32)
        left, right = whole_gram(gram_ref[...])
        first = jnp.concatenate([first, left, identity, zeros], axis=0)
        second = jnp.concatenate([second, right, zeros, identity], axis=0)
    first, second = rotated_halves(skew, inner, first, second)
    staying = jnp.where(moves_second, first, second)
    moving = jnp.where(moves_second, second, first)
    staying_ref, *outs = refs
    staying_ref[...] = staying[:rows]
    if last:
        energies = [
            jnp.sum(half[rows : rows + 2 * width] * half[rows + 2 * width :], axis=0, keepdims=True)
            for half in (staying, moving)
        ]
        outs[-1][...] = jnp.concatenate(energies + [jnp.zeros((6, width), F32)], axis=0)
    if known < rows:
        outs[0][...] = moving[known:rows]
    if known < kept:
        outs[1 if known < rows else 0][...] = staying[known:kept]


def inverse_kernel(s_ref, inner_ref, error_ref, total_ref):
    inner_ref[...] = inverse(s_ref[: s_ref.shape[1]], error_ref, total_ref)


def turned(s_ref, inner_ref, refs):
    width = s_ref.shape[1]
    if len(refs) == 1:
        first, second = refs[0][:, :width], refs[0][:, width:]
    else:
        second = refs[1][...]
        first = jnp.concatenate([refs[0][...]] + [ref[...] for ref in refs[2:]], axis=0)
    first, second = rotated_halves(s_ref[:width], inner_ref[...], first, second)
    moves_second = s_ref[width : width + 1] > 0.5
    return jnp.where(moves_second, second, first), jnp.where(moves_second, first, second)


def joined(staying, moving, pair_ref, *gram_ref):
    width = staying.shape[1]
    pair_ref[:, :width] = staying
    pair_ref[:, width:] = moving
    for ref in gram_ref:
        ref[...] = gram_of(staying, moving, ref.shape[0] > width + 8)


def turn_kernel(parts, s_ref, inner_ref, *refs):
    moving, staying = turned(s_ref, inner_ref, refs[:parts])
    refs[parts][...] = moving
    if len(refs) > parts + 1:
        refs[parts + 1][...] = staying[: refs[parts + 1].shape[0]]


def join_kernel(kept, staying_ref, moving_ref, tail_ref, pair_ref, *outs):
    moving = jnp.concatenate([moving_ref[...], tail_ref[...]], axis=0)
    joined(staying_ref[...], moving, pair_ref, *outs[:1])
    if kept:
        outs[1][...] = moving[:kept]


def turn_join_kernel(kept, parts, s_ref, inner_ref, staying_ref, *refs):
    moving, neighbour_staying = turned(s_ref, inner_ref, refs[:parts])
    pair_ref, *outs = refs[parts:]
    joined(staying_ref[...], moving, pair_ref, *outs[:1])
    if kept:
        outs[1][...] = moving[:kept]
        outs[2][...] = neighbour_staying[: outs[2].shape[0]]


def call(kernel, operands, outs, scratch=(), name="", last=False):
    micros = 0.0 if last else MICROS.get(name, 0.0)
    return pl.pallas_call(
        kernel,
        out_shape=[jax.ShapeDtypeStruct(shape, F32) for shape in outs],
        in_specs=[VMEM] * len(operands),
        out_specs=[VMEM] * len(outs),
        scratch_shapes=list(scratch),
        compiler_params=pltpu.CompilerParams(vmem_limit_bytes=48 * 1024 * 1024),
        cost_estimate=pl.CostEstimate(flops=int(micros * 1e9) + 1, bytes_accessed=int(micros * 3.5e6) + 1, transcendentals=0),
        name=name,
    )(*operands)


def passed_along(block, axis):
    size = lax.axis_size(axis)
    return lax.ppermute(block, axis, [(i, (i + 1) % size) for i in range(size)])


def parts_of_sum(term, axis):
    size = lax.axis_size(axis)
    if size & (size - 1):
        return [lax.psum(term, axis)]
    parts, bit = [term], 1
    while bit < size:
        term = functools.reduce(lambda x, y: x + y, parts)
        masks = [bit] if bit == 1 or 2 * bit >= size else [bit, 2 * bit, 3 * bit]
        parts = [term] + [lax.ppermute(term, axis, [(i, i ^ mask) for i in range(size)]) for mask in masks]
        bit *= 2 if len(masks) == 1 else 4
    return parts


def known_rows(rows, rounds):
    sixteenths = [9, 12] + [14] * rounds
    return [rows * part // 256 * 16 for part in sixteenths[:rounds]] + [0]


def body(record, plan):
    rows, width = record.shape[0], record.shape[1] // 2
    rounds = plan.shape[0]
    total_rows = rows * lax.axis_size("tm")
    square, ratios = (width, width), (width + 8, width)
    grams = [ratios] * (rounds - 1) + [(2 * width + 8, width)]
    scratch = [pltpu.VMEM(square, F32)] * 2
    heads = known_rows(rows, rounds)
    pair = record
    terms, raw_head = call(gram_kernel, [pair], [grams[0], (heads[0], 2 * width)], name="gram")
    neighbour = [passed_along(raw_head, "col")]
    plan_rows = jnp.repeat(jnp.broadcast_to(plan.astype(F32), (rounds, width)), 8, axis=0)
    for step in range(rounds):
        known, kept, last = heads[step], heads[step + 1], step + 1 == rounds
        parts = parts_of_sum(terms, "tm")
        kernel = functools.partial(ratio_kernel, 8 * step, len(parts))
        ratio, *gram = call(kernel, [plan_rows] + parts, [ratios] + [grams[step]] * last, name="ratio", last=last)
        neighbour_ratio = passed_along(ratio, "col")
        outs = [(rows, width)] + [(rows - known, width)] * (known < rows) + [(kept - known, width)] * (known < kept)
        kernel = functools.partial(own_kernel, known, kept, last)
        staying, *sent = call(kernel, [ratio, pair] + gram, outs + [(8, width)] * last, scratch, name="own", last=last)
        (inner,) = call(inverse_kernel, [neighbour_ratio], [square], scratch, name="inverse", last=last)
        turn = [neighbour_ratio, inner]
        sums = [] if last else [grams[step + 1]]
        kept_outs = [(kept, width)] * (kept > 0)
        known_outs = [(min(known, kept), width)] * (kept > 0)
        if known < rows:
            tail = passed_along(sent[0], "col")
            kernel = functools.partial(turn_kernel, len(neighbour))
            moving, *kept_staying = call(kernel, turn + neighbour, [(known, width)] + known_outs, name="turn", last=last)
            if last:
                passed = passed_along(sent[-1], "col")
                moving, passed = lax.optimization_barrier((moving, passed))
            kernel = functools.partial(join_kernel, kept)
            pair, *rest = call(kernel, [staying, moving, tail], [record.shape] + sums + kept_outs, name="join", last=last)
        else:
            tail = None
            if last:
                passed = passed_along(sent[-1], "col")
            kernel = functools.partial(turn_join_kernel, kept, len(neighbour))
            pair, *rest = call(kernel, turn + [staying] + neighbour, [record.shape] + sums + kept_outs + known_outs, name="both", last=last)
            rest, kept_staying = rest[:2], rest[2:]
        if last:
            energy = jnp.concatenate([sent[-1][0], passed[1]])
            return (pair, jnp.sqrt(jnp.maximum(energy, 0.0) / total_rows + epsilon))
        terms, moving = rest
        neighbour = kept_staying + [passed_along(moving, "col")]
        if known < kept:
            more = sent[-1]
            if tail is not None:
                more, _ = lax.optimization_barrier((more, tail))
            neighbour.append(passed_along(more, "col"))


def solution(mesh):
    in_specs = (P("tm", "col"), P(None, "col"))
    out_specs = (P("tm", "col"), P("col"))
    return jax.shard_map(body, mesh=mesh, in_specs=in_specs, out_specs=out_specs, check_vma=False)
```

```python
import functools
import jax
import jax.numpy as jnp
from jax import lax
from jax.experimental import pallas as pl
from jax.experimental.pallas import tpu as pltpu
from jax.sharding import PartitionSpec as P

epsilon = 1e-06
MICROS = (
    {"own": 1.0, "turn": 4.0},
    {"ratio": 2.0, "own": 0.5, "turn": 1.0, "join": 2.0},
    {"ratio": 1.5, "own": 0.8, "turn": 1.0, "join": 0.5, "both": 2.0},
)
F32 = jnp.float32
BF16 = jnp.bfloat16
NN = (((1,), (0,)), ((), ()))
NT = (((1,), (1,)), ((), ()))
TN = (((0,), (0,)), ((), ()))
VMEM = pl.BlockSpec(memory_space=pltpu.VMEM)


def split(x):
    high = x.astype(BF16)
    return high, (x - high.astype(F32)).astype(BF16)


def product(a, b, dims):
    return lax.dot_general(a, b, dims, preferred_element_type=F32)


def right(b, transposed=False):
    high, low = split(b)
    zeros = jnp.zeros_like(low)
    if transposed:
        return jnp.concatenate([jnp.concatenate([high, high], axis=1), jnp.concatenate([low, zeros], axis=1)], axis=0)
    return jnp.concatenate([jnp.concatenate([high, low], axis=1), jnp.concatenate([high, zeros], axis=1)], axis=0)


def times(a, b, transposed=False):
    both = product(jnp.concatenate(split(a), axis=1), b, NT if transposed else NN)
    half = both.shape[1] // 2
    return both[:, :half] + both[:, half:]


def across(a, b):
    both = product(jnp.concatenate(split(a), axis=1), jnp.concatenate(split(b), axis=1), TN)
    width = a.shape[1]
    return both[:width, :width] + (both[:width, width:] + both[width:, :width])


def identity_of(width):
    shape = (width, width)
    return (lax.broadcasted_iota(jnp.int32, shape, 0) == lax.broadcasted_iota(jnp.int32, shape, 1)).astype(F32)


def gram_of(first, second, whole):
    width = first.shape[1]
    parts = [
        across(first, second),
        jnp.sum(first * first, axis=0, keepdims=True),
        jnp.sum(second * second, axis=0, keepdims=True),
        jnp.zeros((6, width), F32),
    ]
    if whole:
        above, below = triangles(width)
        parts.append(
            jnp.where(above, across(first, first), 0.0)
            + jnp.where(below, across(second, second), 0.0)
        )
    return jnp.concatenate(parts, axis=0)


def triangles(width):
    row = lax.broadcasted_iota(jnp.int32, (width, width), 0)
    column = lax.broadcasted_iota(jnp.int32, (width, width), 1)
    return row < column, row > column


def whole_gram(gram):
    width = gram.shape[1]
    above, below = triangles(width)
    identity = identity_of(width)
    cross, packed = gram[:width], gram[width + 8 :]
    blocks = []
    for triangle, diagonal in ((above, gram[width : width + 1]), (below, gram[width + 1 : width + 2])):
        half = jnp.where(triangle, packed, 0.0)
        blocks.append(half + half.T + identity * diagonal)
    return jnp.concatenate([blocks[0], cross.T], axis=0), jnp.concatenate([cross, blocks[1]], axis=0)


def inverse(skew, error_ref, total_ref):
    width = skew.shape[0]
    identity = identity_of(width)
    square = times(skew, right(skew, True), True)
    bound = jnp.minimum(
        jnp.max(jnp.sum(jnp.abs(square), axis=0, keepdims=True), axis=1, keepdims=True),
        jnp.sqrt(jnp.sum(jnp.sum(square * square, axis=0, keepdims=True), axis=1, keepdims=True)),
    )
    scale = 2.0 / (bound + 2.0)
    error_bound = bound / (bound + 2.0)
    error = (1.0 - scale) * identity - scale * square
    total = scale * identity
    for step in range(4):
        grow = 2.0 / (2.0 - error_bound * error_bound)
        if step == 0:
            total, error = (grow * scale) * (identity + error), times(error, right(error))
        else:
            both = times(jnp.concatenate([error, total], axis=0), right(error))
            total, error = grow * (total + both[width:]), both[:width]
        error = (1.0 - grow) * identity + grow * error
        error_bound = error_bound * error_bound / (2.0 - error_bound * error_bound)
    total_ref[...] = total + times(total, right(identity - total - times(square, right(total))))

    @pl.when(error_bound[0, 0] > 1e-3)
    def _():
        exact = functools.partial(lax.dot_general, precision=lax.Precision.HIGHEST, preferred_element_type=F32)
        square = exact(skew, skew, NT)
        error_ref[...] = (1.0 - scale) * identity - scale * square
        total_ref[...] = scale * identity

        def more(error_bound):
            grow = 2.0 / (2.0 - error_bound * error_bound)
            error, total = error_ref[...], total_ref[...]
            total_ref[...] = grow * (total + exact(total, error, NN))
            error_ref[...] = (1.0 - grow) * identity + grow * exact(error, error, NN)
            return error_bound * error_bound / (2.0 - error_bound * error_bound)

        lax.while_loop(lambda error_bound: error_bound > 1e-4, more, (bound / (bound + 2.0))[0, 0])
        for _ in range(2):
            total = total_ref[...]
            total_ref[...] = total + exact(total, identity - total - exact(square, total, NN), NN)

    return total_ref[...]


def rotated_halves(skew, first, second, error_ref, total_ref):
    mixed = first + times(second, right(skew, True), True)
    mixed = times(mixed, right(inverse(skew, error_ref, total_ref)))
    return 2.0 * mixed - first, second - 2.0 * times(mixed, right(skew))


def gram_kernel(pair_ref, gram_ref):
    width = pair_ref.shape[1] // 2
    gram_ref[...] = gram_of(pair_ref[:, :width], pair_ref[:, width:], gram_ref.shape[0] > width + 8)


def ratio_kernel(row, count, plan_ref, *refs):
    parts, (s_ref, *sum_ref) = refs[:count], refs[count:]
    gram = functools.reduce(lambda x, y: x + y, [ref[...] for ref in parts])
    if sum_ref:
        sum_ref[0][...] = gram
    width = gram.shape[1]
    cross, second_diag = gram[:width], gram[width + 1 : width + 2]
    first_diag = jnp.sum(identity_of(width) * gram[width : width + 1], axis=1, keepdims=True)
    difference = first_diag - second_diag
    s_ref[:width] = (
        cross * difference / (2.0 * (difference * difference + 4.0 * cross * cross + 0.01 * first_diag * second_diag))
    )
    s_ref[width:] = plan_ref[row : row + 8]


def own_kernel(known, kept, last, s_ref, pair_ref, *refs):
    *refs, error_ref, total_ref = refs
    width = s_ref.shape[1]
    rows = pair_ref.shape[0]
    skew = s_ref[:width]
    moves_second = s_ref[width : width + 1] > 0.5
    first, second = pair_ref[:, :width], pair_ref[:, width:]
    if last:
        gram_ref, *refs = refs
        identity, zeros = identity_of(width), jnp.zeros((width, width), F32)
        left, right = whole_gram(gram_ref[...])
        first = jnp.concatenate([first, left, identity, zeros], axis=0)
        second = jnp.concatenate([second, right, zeros, identity], axis=0)
    first, second = rotated_halves(skew, first, second, error_ref, total_ref)
    staying = jnp.where(moves_second, first, second)
    moving = jnp.where(moves_second, second, first)
    staying_ref, *outs = refs
    staying_ref[...] = staying[:rows]
    if last:
        energies = [
            jnp.sum(half[rows : rows + 2 * width] * half[rows + 2 * width :], axis=0, keepdims=True)
            for half in (staying, moving)
        ]
        energies = jnp.concatenate(energies + [jnp.zeros((6, width), F32)], axis=0)
        outs[-1][...] = energies
        outs[0][...] = jnp.concatenate([moving[known:rows], energies], axis=0) if known < rows else energies
    elif known < rows:
        outs[0][...] = moving[known:rows]
    if known < kept:
        outs[1 if known < rows else 0][...] = staying[known:kept]


def turned(s_ref, refs, error_ref, total_ref):
    width = s_ref.shape[1]
    if len(refs) == 1:
        first, second = refs[0][:, :width], refs[0][:, width:]
    else:
        second = refs[1][...]
        first = jnp.concatenate([refs[0][...]] + [ref[...] for ref in refs[2:]], axis=0)
    first, second = rotated_halves(s_ref[:width], first, second, error_ref, total_ref)
    moves_second = s_ref[width : width + 1] > 0.5
    return jnp.where(moves_second, second, first), jnp.where(moves_second, first, second)


def joined(staying, moving, pair_ref, *gram_ref):
    width = staying.shape[1]
    pair_ref[:, :width] = staying
    pair_ref[:, width:] = moving
    for ref in gram_ref:
        ref[...] = gram_of(staying, moving, ref.shape[0] > width + 8)


def turn_kernel(parts, s_ref, *refs):
    *refs, error_ref, total_ref = refs
    moving, staying = turned(s_ref, refs[:parts], error_ref, total_ref)
    refs[parts][...] = moving
    if len(refs) > parts + 1:
        refs[parts + 1][...] = staying[: refs[parts + 1].shape[0]]


def column_rms(total_rows, own, passed, rms_ref):
    energy = jnp.concatenate([own[:1], passed[1:2]], axis=1)
    rms_ref[...] = jnp.sqrt(jnp.maximum(energy, 0.0) / total_rows + epsilon)


def join_kernel(kept, total_rows, staying_ref, moving_ref, tail_ref, *refs):
    rows = staying_ref.shape[0]
    known = moving_ref.shape[0]
    moving = jnp.concatenate([moving_ref[...], tail_ref[: rows - known]], axis=0)
    if kept:
        pair_ref, gram_ref, moving_out_ref = refs
        joined(staying_ref[...], moving, pair_ref, gram_ref)
        moving_out_ref[...] = moving[:kept]
    else:
        energies_ref, pair_ref, rms_ref = refs
        joined(staying_ref[...], moving, pair_ref)
        column_rms(total_rows, energies_ref[...], tail_ref[rows - known :], rms_ref)


def turn_join_kernel(kept, total_rows, parts, s_ref, *refs):
    *refs, error_ref, total_ref = refs
    moving, neighbour_staying = turned(s_ref, refs[:parts], error_ref, total_ref)
    staying_ref, *refs = refs[parts:]
    if not kept:
        column_rms(total_rows, refs[0][...], refs[1][...], refs[-1])
        refs = refs[2:-1]
    pair_ref, *outs = refs
    joined(staying_ref[...], moving, pair_ref, *outs[:1])
    if kept:
        outs[1][...] = moving[:kept]
        outs[2][...] = neighbour_staying[: outs[2].shape[0]]


def call(kernel, operands, outs, scratch=(), name="", place=0):
    micros = MICROS[place].get(name, 0.0)
    return pl.pallas_call(
        kernel,
        out_shape=[jax.ShapeDtypeStruct(shape, F32) for shape in outs],
        in_specs=[VMEM] * len(operands),
        out_specs=[VMEM] * len(outs),
        scratch_shapes=list(scratch),
        compiler_params=pltpu.CompilerParams(vmem_limit_bytes=48 * 1024 * 1024),
        cost_estimate=pl.CostEstimate(flops=int(micros * 1e9) + 1, bytes_accessed=int(micros * 3.5e6) + 1, transcendentals=0),
        name=name,
    )(*operands)


def passed_along(block, axis):
    size = lax.axis_size(axis)
    return lax.ppermute(block, axis, [(i, (i + 1) % size) for i in range(size)])


def parts_of_sum(term, axis):
    size = lax.axis_size(axis)
    if size & (size - 1):
        return [lax.psum(term, axis)]
    parts, bit = [term], 1
    while bit < size:
        term = functools.reduce(lambda x, y: x + y, parts)
        masks = [bit] if bit == 1 or 2 * bit >= size else [bit, 2 * bit, 3 * bit]
        parts = [term] + [lax.ppermute(term, axis, [(i, i ^ mask) for i in range(size)]) for mask in masks]
        bit *= 2 if len(masks) == 1 else 4
    return parts


def known_rows(rows, rounds):
    sixteenths = [9, 12] + [14] * rounds
    return [rows * part // 256 * 16 for part in sixteenths[:rounds]] + [0]


def body(record, plan):
    rows, width = record.shape[0], record.shape[1] // 2
    rounds = plan.shape[0]
    total_rows = rows * lax.axis_size("tm")
    square, ratios = (width, width), (width + 8, width)
    grams = [ratios] * (rounds - 1) + [(2 * width + 8, width)]
    scratch = [pltpu.VMEM(square, F32)] * 2
    heads = known_rows(rows, rounds)
    pair = record
    neighbour = [passed_along(record[: heads[0]], "col")]
    (terms,) = call(gram_kernel, [pair], [grams[0]], name="gram")
    plan_rows = jnp.repeat(jnp.broadcast_to(plan.astype(F32), (rounds, width)), 8, axis=0)
    for step in range(rounds):
        known, kept, last = heads[step], heads[step + 1], step + 1 == rounds
        place = 2 if last else min(step, 1)
        parts = parts_of_sum(terms, "tm")
        kernel = functools.partial(ratio_kernel, 8 * step, len(parts))
        ratio, *gram = call(kernel, [plan_rows] + parts, [ratios] + [grams[step]] * last, name="ratio", place=place)
        neighbour_ratio = passed_along(ratio, "col")
        sent_rows = rows - known + 8 * last
        outs = [(rows, width)] + [(sent_rows, width)] * (sent_rows > 0) + [(kept - known, width)] * (known < kept)
        kernel = functools.partial(own_kernel, known, kept, last)
        staying, *sent = call(kernel, [ratio, pair] + gram, outs + [(8, width)] * last, scratch, name="own", place=place)
        tail = passed_along(sent[0], "col") if sent_rows else None
        outs = [record.shape] + ([(1, 2 * width)] if last else [grams[step + 1], (kept, width)])
        known_outs = [(min(known, kept), width)] * (not last)
        if known < rows:
            kernel = functools.partial(turn_kernel, len(neighbour))
            moving, *kept_staying = call(
                kernel, [neighbour_ratio] + neighbour, [(known, width)] + known_outs, scratch, name="turn", place=place
            )
            kernel = functools.partial(join_kernel, kept, total_rows)
            pair, *rest = call(kernel, [staying, moving, tail] + [sent[-1]] * last, outs, name="join", place=place)
        else:
            kernel = functools.partial(turn_join_kernel, kept, total_rows, len(neighbour))
            operands = [neighbour_ratio] + neighbour + [staying] + ([sent[-1], tail] if last else [])
            pair, *rest = call(kernel, operands, outs + known_outs, scratch, name="both", place=place)
            rest, kept_staying = rest[:2], rest[2:]
        if last:
            return (pair, rest[0].reshape(2 * width))
        terms, moving = rest
        neighbour = kept_staying + [passed_along(moving, "col")]
        if known < kept:
            more = sent[-1]
            if tail is not None:
                more, _ = lax.optimization_barrier((more, tail))
            neighbour.append(passed_along(more, "col"))


def solution(mesh):
    in_specs = (P("tm", "col"), P(None, "col"))
    out_specs = (P("tm", "col"), P("col"))
    return jax.shard_map(body, mesh=mesh, in_specs=in_specs, out_specs=out_specs, check_vma=False)
```

```python
import functools
import jax
import jax.numpy as jnp
from jax import lax
from jax.experimental import pallas as pl
from jax.experimental.pallas import tpu as pltpu
from jax.sharding import PartitionSpec as P

epsilon = 1e-06
MICROS = (
    {"own": 1.0, "turn": 2.0},
    {"ratio": 2.0, "own": 0.5, "turn": 1.0, "join": 2.0},
    {"ratio": 1.5, "own": 0.8, "turn": 1.0, "join": 0.5, "both": 2.0},
)
F32 = jnp.float32
BF16 = jnp.bfloat16
NN = (((1,), (0,)), ((), ()))
NT = (((1,), (1,)), ((), ()))
TN = (((0,), (0,)), ((), ()))
VMEM = pl.BlockSpec(memory_space=pltpu.VMEM)


def split(x):
    high = x.astype(BF16)
    return high, (x - high.astype(F32)).astype(BF16)


def product(a, b, dims):
    return lax.dot_general(a, b, dims, preferred_element_type=F32)


def right(b, transposed=False):
    high, low = split(b)
    zeros = jnp.zeros_like(low)
    if transposed:
        return jnp.concatenate([jnp.concatenate([high, high], axis=1), jnp.concatenate([low, zeros], axis=1)], axis=0)
    return jnp.concatenate([jnp.concatenate([high, low], axis=1), jnp.concatenate([high, zeros], axis=1)], axis=0)


def times(a, b, transposed=False):
    both = product(jnp.concatenate(split(a), axis=1), b, NT if transposed else NN)
    half = both.shape[1] // 2
    return both[:, :half] + both[:, half:]


def across(a, b):
    both = product(jnp.concatenate(split(a), axis=1), jnp.concatenate(split(b), axis=1), TN)
    width = a.shape[1]
    return both[:width, :width] + (both[:width, width:] + both[width:, :width])


def identity_of(width):
    shape = (width, width)
    return (lax.broadcasted_iota(jnp.int32, shape, 0) == lax.broadcasted_iota(jnp.int32, shape, 1)).astype(F32)


def gram_of(first, second, whole):
    width = first.shape[1]
    parts = [
        across(first, second),
        jnp.sum(first * first, axis=0, keepdims=True),
        jnp.sum(second * second, axis=0, keepdims=True),
        jnp.zeros((6, width), F32),
    ]
    if whole:
        above, below = triangles(width)
        parts.append(
            jnp.where(above, across(first, first), 0.0)
            + jnp.where(below, across(second, second), 0.0)
        )
    return jnp.concatenate(parts, axis=0)


def triangles(width):
    row = lax.broadcasted_iota(jnp.int32, (width, width), 0)
    column = lax.broadcasted_iota(jnp.int32, (width, width), 1)
    return row < column, row > column


def whole_gram(gram):
    width = gram.shape[1]
    above, below = triangles(width)
    identity = identity_of(width)
    cross, packed = gram[:width], gram[width + 8 :]
    blocks = []
    for triangle, diagonal in ((above, gram[width : width + 1]), (below, gram[width + 1 : width + 2])):
        half = jnp.where(triangle, packed, 0.0)
        blocks.append(half + half.T + identity * diagonal)
    return jnp.concatenate([blocks[0], cross.T], axis=0), jnp.concatenate([cross, blocks[1]], axis=0)


def inverse(skew, error_ref, total_ref):
    width = skew.shape[0]
    identity = identity_of(width)
    square = times(skew, right(skew, True), True)
    bound = jnp.minimum(
        jnp.max(jnp.sum(jnp.abs(square), axis=0, keepdims=True), axis=1, keepdims=True),
        jnp.sqrt(jnp.sum(jnp.sum(square * square, axis=0, keepdims=True), axis=1, keepdims=True)),
    )
    scale = 2.0 / (bound + 2.0)
    error_bound = bound / (bound + 2.0)
    error = (1.0 - scale) * identity - scale * square
    total = scale * identity
    for step in range(4):
        grow = 2.0 / (2.0 - error_bound * error_bound)
        if step == 0:
            total, error = (grow * scale) * (identity + error), times(error, right(error))
        else:
            both = times(jnp.concatenate([error, total], axis=0), right(error))
            total, error = grow * (total + both[width:]), both[:width]
        error = (1.0 - grow) * identity + grow * error
        error_bound = error_bound * error_bound / (2.0 - error_bound * error_bound)
    total_ref[...] = total + times(total, right(identity - total - times(square, right(total))))

    @pl.when(error_bound[0, 0] > 1e-3)
    def _():
        exact = functools.partial(lax.dot_general, precision=lax.Precision.HIGHEST, preferred_element_type=F32)
        square = exact(skew, skew, NT)
        error_ref[...] = (1.0 - scale) * identity - scale * square
        total_ref[...] = scale * identity

        def more(error_bound):
            grow = 2.0 / (2.0 - error_bound * error_bound)
            error, total = error_ref[...], total_ref[...]
            total_ref[...] = grow * (total + exact(total, error, NN))
            error_ref[...] = (1.0 - grow) * identity + grow * exact(error, error, NN)
            return error_bound * error_bound / (2.0 - error_bound * error_bound)

        lax.while_loop(lambda error_bound: error_bound > 1e-4, more, (bound / (bound + 2.0))[0, 0])
        for _ in range(2):
            total = total_ref[...]
            total_ref[...] = total + exact(total, identity - total - exact(square, total, NN), NN)

    return total_ref[...]


def rotated_halves(skew, first, second, error_ref, total_ref):
    mixed = first + times(second, right(skew, True), True)
    mixed = times(mixed, right(inverse(skew, error_ref, total_ref)))
    return 2.0 * mixed - first, second - 2.0 * times(mixed, right(skew))


def gram_kernel(pair_ref, gram_ref):
    width = pair_ref.shape[1] // 2
    gram_ref[...] = gram_of(pair_ref[:, :width], pair_ref[:, width:], gram_ref.shape[0] > width + 8)


def ratio_kernel(row, count, plan_ref, *refs):
    parts, (s_ref, *sum_ref) = refs[:count], refs[count:]
    gram = functools.reduce(lambda x, y: x + y, [ref[...] for ref in parts])
    if sum_ref:
        sum_ref[0][...] = gram
    width = gram.shape[1]
    cross, second_diag = gram[:width], gram[width + 1 : width + 2]
    first_diag = jnp.sum(identity_of(width) * gram[width : width + 1], axis=1, keepdims=True)
    difference = first_diag - second_diag
    s_ref[:width] = (
        cross * difference / (2.0 * (difference * difference + 4.0 * cross * cross + 0.01 * first_diag * second_diag))
    )
    s_ref[width:] = plan_ref[row : row + 8]


def own_kernel(known, kept, last, s_ref, pair_ref, *refs):
    *refs, error_ref, total_ref = refs
    width = s_ref.shape[1]
    rows = pair_ref.shape[0]
    skew = s_ref[:width]
    moves_second = s_ref[width : width + 1] > 0.5
    first, second = pair_ref[:, :width], pair_ref[:, width:]
    if last:
        gram_ref, *refs = refs
        identity, zeros = identity_of(width), jnp.zeros((width, width), F32)
        left, right = whole_gram(gram_ref[...])
        first = jnp.concatenate([first, left, identity, zeros], axis=0)
        second = jnp.concatenate([second, right, zeros, identity], axis=0)
    first, second = rotated_halves(skew, first, second, error_ref, total_ref)
    staying = jnp.where(moves_second, first, second)
    moving = jnp.where(moves_second, second, first)
    staying_ref, *outs = refs
    staying_ref[...] = staying[:rows]
    if last:
        energies = [
            jnp.sum(half[rows : rows + 2 * width] * half[rows + 2 * width :], axis=0, keepdims=True)
            for half in (staying, moving)
        ]
        energies = jnp.concatenate(energies + [jnp.zeros((6, width), F32)], axis=0)
        outs[-1][...] = energies
        outs[0][...] = jnp.concatenate([moving[known:rows], energies], axis=0) if known < rows else energies
    elif known < rows:
        outs[0][...] = moving[known:rows]
    if known < kept:
        outs[1 if known < rows else 0][...] = staying[known:kept]


def turned(s_ref, refs, error_ref, total_ref):
    width = s_ref.shape[1]
    if len(refs) == 1:
        first, second = refs[0][:, :width], refs[0][:, width:]
    else:
        second = refs[1][...]
        first = jnp.concatenate([refs[0][...]] + [ref[...] for ref in refs[2:]], axis=0)
    first, second = rotated_halves(s_ref[:width], first, second, error_ref, total_ref)
    moves_second = s_ref[width : width + 1] > 0.5
    return jnp.where(moves_second, second, first), jnp.where(moves_second, first, second)


def joined(staying, moving, pair_ref, *gram_ref):
    width = staying.shape[1]
    pair_ref[:, :width] = staying
    pair_ref[:, width:] = moving
    for ref in gram_ref:
        ref[...] = gram_of(staying, moving, ref.shape[0] > width + 8)


def turn_kernel(parts, s_ref, *refs):
    *refs, error_ref, total_ref = refs
    moving, staying = turned(s_ref, refs[:parts], error_ref, total_ref)
    refs[parts][...] = moving
    if len(refs) > parts + 1:
        refs[parts + 1][...] = staying[: refs[parts + 1].shape[0]]


def column_rms(total_rows, own, passed, rms_ref):
    energy = jnp.concatenate([own[:1], passed[1:2]], axis=1)
    rms_ref[...] = jnp.sqrt(jnp.maximum(energy, 0.0) / total_rows + epsilon)


def join_kernel(kept, total_rows, staying_ref, moving_ref, tail_ref, *refs):
    rows = staying_ref.shape[0]
    known = moving_ref.shape[0]
    moving = jnp.concatenate([moving_ref[...], tail_ref[: rows - known]], axis=0)
    if kept:
        pair_ref, gram_ref, moving_out_ref = refs
        joined(staying_ref[...], moving, pair_ref, gram_ref)
        moving_out_ref[...] = moving[:kept]
    else:
        energies_ref, pair_ref, rms_ref = refs
        joined(staying_ref[...], moving, pair_ref)
        column_rms(total_rows, energies_ref[...], tail_ref[rows - known :], rms_ref)


def turn_join_kernel(kept, total_rows, parts, s_ref, *refs):
    *refs, error_ref, total_ref = refs
    moving, neighbour_staying = turned(s_ref, refs[:parts], error_ref, total_ref)
    staying_ref, *refs = refs[parts:]
    if not kept:
        column_rms(total_rows, refs[0][...], refs[1][...], refs[-1])
        refs = refs[2:-1]
    pair_ref, *outs = refs
    joined(staying_ref[...], moving, pair_ref, *outs[:1])
    if kept:
        outs[1][...] = moving[:kept]
        outs[2][...] = neighbour_staying[: outs[2].shape[0]]


def call(kernel, operands, outs, scratch=(), name="", place=0):
    micros = MICROS[place].get(name, 0.0)
    return pl.pallas_call(
        kernel,
        out_shape=[jax.ShapeDtypeStruct(shape, F32) for shape in outs],
        in_specs=[VMEM] * len(operands),
        out_specs=[VMEM] * len(outs),
        scratch_shapes=list(scratch),
        compiler_params=pltpu.CompilerParams(vmem_limit_bytes=48 * 1024 * 1024),
        cost_estimate=pl.CostEstimate(flops=int(micros * 1e9) + 1, bytes_accessed=int(micros * 3.5e6) + 1, transcendentals=0),
        name=name,
    )(*operands)


def passed_along(block, axis):
    size = lax.axis_size(axis)
    return lax.ppermute(block, axis, [(i, (i + 1) % size) for i in range(size)])


def parts_of_sum(term, axis, ahead):
    size = lax.axis_size(axis)
    if size & (size - 1):
        return [lax.psum(term, axis)], ahead
    parts, bit = [term], 1
    while bit < size:
        term = functools.reduce(lambda x, y: x + y, parts)
        if bit > 1:
            term, ahead = lax.optimization_barrier((term, ahead))
        masks = [bit] if bit == 1 or 2 * bit >= size else [bit, 2 * bit, 3 * bit]
        parts = [term] + [lax.ppermute(term, axis, [(i, i ^ mask) for i in range(size)]) for mask in masks]
        bit *= 2 if len(masks) == 1 else 4
    return parts, ahead


def known_rows(rows, rounds):
    sixteenths = [9, 12] + [14] * rounds
    return [rows * part // 256 * 16 for part in sixteenths[:rounds]] + [0]


def body(record, plan):
    rows, width = record.shape[0], record.shape[1] // 2
    rounds = plan.shape[0]
    total_rows = rows * lax.axis_size("tm")
    square, ratios = (width, width), (width + 8, width)
    grams = [ratios] * (rounds - 1) + [(2 * width + 8, width)]
    scratch = [pltpu.VMEM(square, F32)] * 2
    heads = known_rows(rows, rounds)
    pair = record
    neighbour = [passed_along(record[: heads[0]], "col")]
    (terms,) = call(gram_kernel, [pair], [grams[0]], name="gram")
    plan_rows = jnp.repeat(jnp.broadcast_to(plan.astype(F32), (rounds, width)), 8, axis=0)
    ahead = []
    for step in range(rounds):
        known, kept, last = heads[step], heads[step + 1], step + 1 == rounds
        place = 2 if last else min(step, 1)
        parts, ahead = parts_of_sum(terms, "tm", ahead)
        neighbour += ahead
        kernel = functools.partial(ratio_kernel, 8 * step, len(parts))
        ratio, *gram = call(kernel, [plan_rows] + parts, [ratios] + [grams[step]] * last, name="ratio", place=place)
        neighbour_ratio = passed_along(ratio, "col")
        sent_rows = rows - known + 8 * last
        outs = [(rows, width)] + [(sent_rows, width)] * (sent_rows > 0) + [(kept - known, width)] * (known < kept)
        kernel = functools.partial(own_kernel, known, kept, last)
        staying, *sent = call(kernel, [ratio, pair] + gram, outs + [(8, width)] * last, scratch, name="own", place=place)
        tail = passed_along(sent[0], "col") if sent_rows else None
        outs = [record.shape] + ([(1, 2 * width)] if last else [grams[step + 1], (kept, width)])
        known_outs = [(min(known, kept), width)] * (not last)
        if known < rows:
            kernel = functools.partial(turn_kernel, len(neighbour))
            moving, *kept_staying = call(
                kernel, [neighbour_ratio] + neighbour, [(known, width)] + known_outs, scratch, name="turn", place=place
            )
            kernel = functools.partial(join_kernel, kept, total_rows)
            pair, *rest = call(kernel, [staying, moving, tail] + [sent[-1]] * last, outs, name="join", place=place)
        else:
            kernel = functools.partial(turn_join_kernel, kept, total_rows, len(neighbour))
            operands = [neighbour_ratio] + neighbour + [staying] + ([sent[-1], tail] if last else [])
            pair, *rest = call(kernel, operands, outs + known_outs, scratch, name="both", place=place)
            rest, kept_staying = rest[:2], rest[2:]
        if last:
            return (pair, rest[0].reshape(2 * width))
        terms, moving = rest
        neighbour = kept_staying + [passed_along(moving, "col")]
        ahead = []
        if known < kept and step == 0:
            ahead = [passed_along(sent[-1], "col")]
        elif known < kept:
            more = sent[-1]
            if tail is not None:
                more, _ = lax.optimization_barrier((more, tail))
            neighbour.append(passed_along(more, "col"))


def solution(mesh):
    in_specs = (P("tm", "col"), P(None, "col"))
    out_specs = (P("tm", "col"), P("col"))
    return jax.shard_map(body, mesh=mesh, in_specs=in_specs, out_specs=out_specs, check_vma=False)
```
